32 devices in a mesh: parts: 2 (over y), tensor: 4 (over z), example: 4 (over x, core).
Axes of the slice: x: 2, y: 2, z: 4, core: 2. Of those that a mesh axis runs over, the one named last changes fastest.
Arguments:
- activations: bfloat16 [48, 512, 28672], P(('parts', 'example'), None, 'tensor'), parts along dimension 0, may hold values from -6 to 6
- out_grads: bfloat16 [48, 512, 8192], P(('parts', 'example'), None, 'tensor'), parts along dimension 0, may hold values from -6 to 6
- lengths: int32 [48], P(('parts', 'example')), parts along dimension 0, may hold values from 1 to 512, 9216 in all
- proj_in: bfloat16 [28672, 64], P('tensor'), may hold values from -2.362278 to 2.362278
- proj_out: bfloat16 [8192, 64], P('tensor'), may hold values from -4.4194174 to 4.4194174
- queries: bfloat16 [8192, 4096], P(('parts', 'example'), 'tensor'), parts along dimension 0, may hold values from -6 to 6
Outputs:
- scores: float32 [48, 4096], P(('parts', 'example'), 'tensor'), parts along dimension 0
The draws below stay inside these ranges and needn't reach their ends.
There are 2 independent parts, one for each index of `parts`. The reference program is written for one: setup_inputs(seed, part) draws one part's arguments, and reference() takes and returns one part's arrays. A program takes and returns all parts, laid end to end along the dimension named above; an argument that names none is the same for every part. Nothing has to cross between parts.
All inputs are finite; a program needn't handle non-finite values. No bound on the sum of `lengths` on one device may be relied on, other than what follows from the above.
Results may differ from the reference program's by a relative error of at most 0.0029.
Values may be sent and summed in bfloat16 or wider, within the bound.
No kernel may reach another device: no remote copies, remote signals or barrier semaphores. Data moves between devices by JAX's collectives and lax.ppermute only.
A program may use at most 192 MiB of HBM per device.

```python
import math
import jax
import jax.numpy as jnp
import numpy as np
from jax import lax

D = 8192
FF = 28672
RANK = 64
LEN = 512
Q = 4096
LISTS = 24


def basis_draw(key, rows, cols, spread_rising):
    first, second, third = jax.random.split(key, 3)
    base = jnp.clip(jax.random.normal(first, (rows, cols), jnp.float32), -6.0, 6.0)
    rough = jnp.exp(jax.random.uniform(second, (1, cols), jnp.float32, jnp.log(0.5), jnp.log(2.0)))
    if spread_rising > 0:
        column_scale = 10.0 ** (jnp.arange(cols, dtype=jnp.float32) / (cols - 1))
        rough = rough * column_scale[None, :]
    else:
        rough = rough * jnp.exp(jax.random.uniform(third, (1, cols), jnp.float32, 0.0, jnp.log(10.0)))
    return base * rough / jnp.sqrt(jnp.float32(rows))


def draw_proj_in(key, part):
    key = jax.random.fold_in(key, 11)
    return basis_draw(key, FF, RANK, 1).astype(jnp.bfloat16)


def draw_proj_out(key, part):
    key = jax.random.fold_in(key, 23)
    return basis_draw(key, D, RANK, 0).astype(jnp.bfloat16)


def strengthened(drawn, own_key, source, target, shards_of, factor):
    def block_of(dim):
        return (jnp.arange(drawn.shape[dim]) // (drawn.shape[dim] // shards_of)).reshape((-1,) + (1,) * (drawn.ndim - 1 - dim))

    one_side = jax.random.permutation(own_key, shards_of)[block_of(target)]
    far = (block_of(target) + shards_of // 2) % shards_of
    return jnp.where((block_of(source) == one_side) | (block_of(source) == far), factor * drawn, drawn)


def block_levels(key, dims, cuts, low, top_value):
    def one(position, blocks):
        draws = jax.random.uniform(jax.random.fold_in(jax.random.fold_in(key, 6), position), (blocks,), jnp.float32, low / len(cuts), top_value / len(cuts))
        return jnp.repeat(jnp.exp(draws), dims[position] // blocks).reshape((-1,) + (1,) * (len(dims) - position - 1))

    loudness = one(*cuts[0])
    for cut in cuts[1:]:
        loudness = loudness * one(*cut)
    return loudness


def length_profile(count, total, limit, lean):
    weights = [(1 << 20) // math.isqrt(standing ** lean) + 1 for standing in range(2, count + 1)]
    surplus, given = total - limit - (count - 1), [1] * (count - 1)
    while surplus > 0:
        movable = [i for i in range(count - 1) if given[i] < limit]
        pool, left = sum([weights[i] for i in movable]), surplus
        for i in movable:
            extra = min(limit - given[i], max(1, left * weights[i] // pool), surplus)
            given[i] = given[i] + extra
            surplus = surplus - extra
    return np.array([limit] + given)


def ragged_sizes(rng, amount, total, reach, skew):
    if amount == 2:
        one = jax.random.randint(rng, (), max(1, total - reach), min(reach, total - 1) + 1)
        return jnp.stack([one, total - one])
    sizes = jnp.asarray(length_profile(amount, total, reach, skew), jnp.int32)
    pairs = (amount - 1) // 2
    donor, taker = sizes[1:1 + 2 * pairs:2], sizes[2:2 + 2 * pairs:2]
    margin = jnp.minimum(donor - 1, reach - taker)
    passed = jax.random.randint(jax.random.fold_in(rng, 1), (pairs,), 0, 1 << 20) % (margin + 1)
    sizes = sizes.at[1:1 + 2 * pairs:2].set(donor - passed).at[2:2 + 2 * pairs:2].set(taker + passed)
    return sizes[jax.random.permutation(jax.random.fold_in(rng, 2), amount)]


def noise(own_key, shape, spread, bound, shards=(), held_as=jnp.bfloat16):
    level = block_levels(own_key, shape, shards, -0.22, 0.18) if shards else 1.0
    entries = jax.random.normal(own_key, shape, jnp.float32) * spread * level
    return jnp.minimum(jnp.maximum(entries, -bound), bound).astype(held_as)


def bell_draw_with(own_key, shape, width, reach, cuts, heavy, kind=jnp.bfloat16):
    drawn = width * jax.random.normal(own_key, shape, jnp.float32)
    if cuts:
        drawn = drawn * block_levels(own_key, shape, cuts, -0.22, 0.18)
    return jnp.clip(strengthened(drawn, jax.random.fold_in(own_key, 3), *heavy), -reach, reach).astype(kind)


def setup_inputs(seed: int = 0, part: int = 0) -> dict:
    keys = jax.random.split(jax.random.key(seed), 7)
    part_keys = jax.random.split(jax.random.fold_in(keys[6], part), 7)
    activations = noise(part_keys[0], (LISTS, LEN, FF), 1.0, 6.0, ((0, 4), (2, 4)))
    out_grads = noise(part_keys[1], (LISTS, LEN, D), 1.0, 6.0, ((0, 4), (2, 4)))
    lengths = ragged_sizes(part_keys[2], LISTS, LISTS * LEN * 3 // 4, LEN, 1).astype(jnp.int32)
    proj_in = draw_proj_in(jax.random.fold_in(keys[6], 71), part)
    proj_out = draw_proj_out(jax.random.fold_in(keys[6], 71), part)
    queries = bell_draw_with(part_keys[5], (Q, RANK * RANK), 1.0, 6.0, ((0, 4), (1, 4)), (1, 0, 4, 2.0))
    return {"activations": activations, "out_grads": out_grads, "lengths": lengths, "proj_in": proj_in, "proj_out": proj_out, "queries": queries}


def reference(activations, out_grads, lengths, proj_in, proj_out, queries):

    def per_list(args):
        acts, grads, count = args
        left = jnp.dot(acts, proj_in, preferred_element_type=jnp.float32)
        right = jnp.dot(grads, proj_out, preferred_element_type=jnp.float32)
        keep = (jnp.arange(LEN, dtype=jnp.int32) < count).astype(jnp.float32)[:, None]
        sketch = jnp.dot((left * keep).T, right, precision=lax.Precision.HIGHEST)
        total = jnp.sum(sketch * sketch)
        return sketch / jnp.sqrt(total + 1e-06)
    units = lax.map(per_list, (activations, out_grads, lengths))
    units = units.reshape(LISTS, RANK * RANK).astype(jnp.bfloat16)
    return lax.dot_general(units, queries, (((1,), (1,)), ((), ())), preferred_element_type=jnp.float32)
```

```python
import functools

import jax
import jax.numpy as jnp
from jax import lax
from jax.experimental import pallas as pl
from jax.experimental.pallas import tpu as pltpu
from jax.sharding import PartitionSpec as P

TOP = 14.0
EXTRA = 8
NT = (((1,), (1,)), ((), ()))
NN = (((1,), (0,)), ((), ()))


def right_kernel(grads, basis, out):
    rank = basis.shape[0]
    right = lax.dot_general(grads[0], basis[...], NT, preferred_element_type=jnp.float32).T
    largest = jnp.max(jnp.abs(right), axis=0, keepdims=True)
    exponent = jnp.ceil(jnp.log2(jnp.maximum(largest, 1e-30)))
    out[:rank] = right * jnp.exp2(TOP - exponent)
    out[rank:] = jnp.broadcast_to(exponent, (EXTRA, right.shape[1]))


def project_right(out_grads, basis):
    lists, slots, width = out_grads.shape
    rank = basis.shape[0]
    return pl.pallas_call(
        right_kernel,
        grid=(lists,),
        in_specs=[
            pl.BlockSpec((1, slots, width), lambda l: (l, 0, 0)),
            pl.BlockSpec((rank, width), lambda l: (0, 0)),
        ],
        out_specs=pl.BlockSpec((rank + EXTRA, slots), lambda l: (0, l)),
        out_shape=jax.ShapeDtypeStruct((rank + EXTRA, lists * slots), jnp.float32),
        cost_estimate=pl.CostEstimate(flops=8 * lists * slots * width * rank, bytes_accessed=2 * out_grads.size, transcendentals=0),
        compiler_params=pltpu.CompilerParams(vmem_limit_bytes=40 << 20),
        name="project_right",
    )(out_grads, basis)


def left_kernel(first, depth, lengths, acts, basis, out, total):
    step = pl.program_id(1)
    rank = basis.shape[0]
    columns = pl.ds(pl.multiple_of(step * depth, depth), depth)
    part = lax.dot_general(acts[0], basis[:, columns], NT, preferred_element_type=jnp.float32)

    @pl.when(step == 0)
    def _():
        total[...] = part

    @pl.when(step > 0)
    def _():
        total[...] += part

    @pl.when(step == pl.num_programs(1) - 1)
    def _():
        count = lengths[pl.program_id(0) + first]
        rows = lax.broadcasted_iota(jnp.int32, total.shape, 0)
        left = jnp.where(rows < count, total[...], 0.0)
        head = left.astype(jnp.bfloat16)
        out[:, :rank] = head
        out[:, rank:] = (left - head.astype(jnp.float32)).astype(jnp.bfloat16)


def project_left(activations, basis, lengths, first, lists, cuts):
    slots, width = activations.shape[1:]
    rank = basis.shape[0]
    depth = width // cuts
    return pl.pallas_call(
        functools.partial(left_kernel, first, depth),
        grid_spec=pltpu.PrefetchScalarGridSpec(
            num_scalar_prefetch=1,
            grid=(lists, cuts),
            in_specs=[
                pl.BlockSpec((1, slots, depth), lambda l, k, _: (l + first, 0, k)),
                pl.BlockSpec((rank, width), lambda l, k, _: (0, 0)),
            ],
            out_specs=pl.BlockSpec((slots, 2 * rank), lambda l, k, _: (l, 0)),
            scratch_shapes=[pltpu.VMEM((slots, rank), jnp.float32)],
        ),
        out_shape=jax.ShapeDtypeStruct((lists * slots, 2 * rank), jnp.bfloat16),
        cost_estimate=pl.CostEstimate(flops=8 * lists * slots * width * rank, bytes_accessed=2 * lists * slots * width, transcendentals=0),
        compiler_params=pltpu.CompilerParams(vmem_limit_bytes=40 << 20),
        name="project_left",
    )(lengths, activations, basis)


def sketch_kernel(unit, per_list, half, where, rights, left_a, left_b, out, sums):
    rank = sums.shape[1]
    width = rights.shape[2]
    sums[...] = jnp.zeros_like(sums)
    for block in range(rights.shape[0]):
        value = rights[block]
        head = value.astype(jnp.bfloat16)
        both = jnp.concatenate([head, (value - head.astype(jnp.float32)).astype(jnp.bfloat16)], axis=0)
        for piece in range(width // unit):
            index = where[block] * (width // unit) + piece
            right = both[:, piece * unit:(piece + 1) * unit]

            def add(left_ref, start):
                left = left_ref[pl.ds(pl.multiple_of(start * unit, unit), unit), :]
                full = lax.dot_general(right, left, NN, preferred_element_type=jnp.float32)
                side = full[:rank] + full[rank:]
                sums[index // per_list] += side[:, :rank] + side[:, rank:]

            @pl.when(index < half)
            def _():
                add(left_a, index)

            @pl.when(index >= half)
            def _():
                add(left_b, index - half)

    for l in range(sums.shape[0]):
        sums[l] = sums[l].T
    rows = out.shape[2] // rank
    for i in range(rank):
        column = (i % rows) * rank
        out[i // rows, :sums.shape[0], column:column + rank] = sums[:, i, :]


def sketch_terms(where, rights, left_a, left_b, lists, slots, groups):
    rank = rights.shape[1]
    unit = slots // 2
    vmem = pl.BlockSpec(memory_space=pltpu.VMEM)
    return pl.pallas_call(
        functools.partial(sketch_kernel, unit, slots // unit, left_a.shape[0] // unit),
        in_specs=[pl.BlockSpec(memory_space=pltpu.SMEM), vmem, vmem, vmem],
        out_specs=vmem,
        out_shape=jax.ShapeDtypeStruct((groups, 8, rank * rank // groups), jnp.float32),
        scratch_shapes=[pltpu.VMEM((lists, rank, rank), jnp.float32)],
        compiler_params=pltpu.CompilerParams(vmem_limit_bytes=40 << 20),
        name="sketch_terms",
    )(where, rights, left_a, left_b)


def score_kernel(*refs):
    sketches, queries, out = refs[:-2], refs[-2], refs[-1]
    count = queries.shape[0]
    value = jnp.concatenate([s[...] for s in sketches], axis=0)
    head = value.astype(jnp.bfloat16)
    both = jnp.concatenate([head, (value - head.astype(jnp.float32)).astype(jnp.bfloat16)], axis=0)
    full = lax.dot_general(both, queries[...], NT, preferred_element_type=jnp.float32)
    rows = value.shape[0]
    terms = full[:rows] + full[rows:]
    squares = jnp.sum(value * value, axis=1, keepdims=True)
    for group in range(len(sketches)):
        out[group, :, :count] = terms[group * 8:group * 8 + 8]
        out[group, :, count:] = jnp.broadcast_to(squares[group * 8:group * 8 + 8], (8, 128))


def score_terms(sketches, queries):
    vmem = pl.BlockSpec(memory_space=pltpu.VMEM)
    return pl.pallas_call(
        score_kernel,
        in_specs=[vmem] * (len(sketches) + 1),
        out_specs=vmem,
        out_shape=jax.ShapeDtypeStruct((len(sketches), 8, queries.shape[0] + 128), jnp.float32),
        compiler_params=pltpu.CompilerParams(vmem_limit_bytes=40 << 20),
        name="score_terms",
    )(*sketches, queries)


def ring(size, shift):
    return [(i, (i + shift) % size) for i in range(size)]


def decoded(coded, rank):
    wide = coded.astype(jnp.float32)
    return wide[..., :rank, :] * jnp.exp2(wide[..., rank:rank + 1, :] - TOP)


def local_square(activations, out_grads, lengths, proj_in, proj_out, queries):
    lists, slots, _ = activations.shape
    rank = proj_in.shape[1]
    groups = lax.axis_size("tensor")
    me = lax.axis_index("tensor")
    shifts = range(1, groups)
    tokens = lists * slots
    block = tokens // groups

    right = project_right(out_grads, proj_out.T)
    coded = right.astype(jnp.float16)

    def part(shift):
        return lax.dynamic_slice_in_dim(coded, (me + shift) % groups * block, block, 1)

    arrived = [lax.ppermute(part(shift), "tensor", ring(groups, shift)) for shift in shifts]
    early = lists // 2
    left_a = project_left(activations, proj_in.T, lengths, 0, early, 2)
    pieces = [part(0)] + arrived
    wide = [p.astype(jnp.float32) for p in pieces]
    summed = sum(w * jnp.exp2(w[rank:rank + 1] - TOP) for w in wide)
    exponent = functools.reduce(jnp.maximum, [w[rank:rank + 1] for w in wide]) + (groups - 1).bit_length()
    row = lax.broadcasted_iota(jnp.int32, summed.shape, 0)
    mine = jnp.where(row < rank, summed * jnp.exp2(TOP - exponent), exponent).astype(jnp.float16)
    blocks = [mine] + [lax.ppermute(mine, "tensor", ring(groups, shift)) for shift in shifts]
    left_b = project_left(activations, proj_in.T, lengths, early, lists - early, 2)
    rights = decoded(jnp.stack(blocks), rank)
    where = (me - jnp.arange(groups, dtype=jnp.int32)) % groups
    terms = sketch_terms(where, rights, left_a, left_b, lists, slots, groups)

    def towards(array, index):
        return lax.dynamic_index_in_dim(array, index, 0, keepdims=False)

    sketch = towards(terms, me)
    for shift in shifts:
        sketch = sketch + lax.ppermute(towards(terms, (me + shift) % groups), "tensor", ring(groups, shift))
    sketches = [sketch] + [lax.ppermute(sketch, "example", ring(groups, shift)) for shift in shifts]
    scores = score_terms(sketches, queries)
    here = lax.axis_index("example")
    final = None
    for shift in range(groups):
        target = (me + shift) % groups
        pairs = [
            (t * groups + e, e * groups + (t + shift) % groups)
            for t in range(groups) for e in range(groups)
        ]
        moved = lax.ppermute(towards(scores, (here - target) % groups), ("tensor", "example"), pairs)
        final = moved if final is None else final + moved
    count = queries.shape[0]
    return final[:lists, :count] * lax.rsqrt(final[:lists, count:count + 1] + 1e-06)


def local(activations, out_grads, lengths, proj_in, proj_out, queries):
    nlists, slots, hidden_width = activations.shape
    feature_width = out_grads.shape[2]
    rank = proj_in.shape[1]
    left_part = jnp.dot(
        activations.reshape(nlists * slots, hidden_width),
        proj_in,
        preferred_element_type=jnp.float32,
    )
    right_part = jnp.dot(
        out_grads.reshape(nlists * slots, feature_width),
        proj_out,
        preferred_element_type=jnp.float32,
    )
    stacked = jnp.concatenate([left_part, right_part], axis=1).reshape(nlists, slots, 2 * rank)
    groups = lax.axis_size("tensor")
    block_rows = rank // groups
    summed = lax.psum(stacked, "tensor")
    positions = lax.broadcasted_iota(jnp.int32, (nlists, slots), 1)
    keep = (positions < lengths[:, None]).astype(jnp.float32)[:, :, None]
    left_full = summed[:, :, :rank] * keep
    right_full = summed[:, :, rank:]
    sketch = jnp.einsum("ltr,lts->lrs", left_full, right_full, precision=lax.Precision.HIGHEST)
    totals = jnp.sum(sketch * sketch, axis=(1, 2))
    unit_all = (sketch / jnp.sqrt(totals + 1e-06)[:, None, None]).astype(jnp.bfloat16)
    first_row = lax.axis_index("tensor") * block_rows
    mine = lax.dynamic_slice_in_dim(unit_all, first_row, block_rows, 1)
    mine = mine.reshape(nlists, block_rows * rank)
    terms = lax.dot_general(
        mine,
        lax.all_gather(queries, "example", axis=0, tiled=True),
        (((1,), (1,)), ((), ())),
        preferred_element_type=jnp.float32,
    )
    return lax.psum_scatter(terms, "tensor", scatter_dimension=1, tiled=True)


def solution(mesh):
    in_specs = (
        P(("parts", "example"), None, "tensor"),
        P(("parts", "example"), None, "tensor"),
        P(("parts", "example")),
        P("tensor", None),
        P("tensor", None),
        P(("parts", "example"), "tensor"),
    )
    out_specs = P(("parts", "example"), "tensor")
    square = mesh.shape["tensor"] == mesh.shape["example"]
    plan = local_square if square else local
    return jax.shard_map(plan, mesh=mesh, in_specs=in_specs, out_specs=out_specs, check_vma=False)
```

```python
import functools

import jax
import jax.numpy as jnp
from jax import lax
from jax.experimental import pallas as pl
from jax.experimental.pallas import tpu as pltpu
from jax.sharding import PartitionSpec as P

TOP = 14.0
EXTRA = 8
UNITS = 4
NT = (((1,), (1,)), ((), ()))
NN = (((1,), (0,)), ((), ()))


def right_kernel(grads, basis, out):
    rank = basis.shape[0]
    right = lax.dot_general(grads[0], basis[...], NT, preferred_element_type=jnp.float32).T
    largest = jnp.max(jnp.abs(right), axis=0, keepdims=True)
    exponent = jnp.ceil(jnp.log2(jnp.maximum(largest, 1e-30)))
    out[:rank] = right * jnp.exp2(TOP - exponent)
    out[rank:] = jnp.broadcast_to(exponent, (EXTRA, right.shape[1]))


def project_right(out_grads, basis):
    lists, slots, width = out_grads.shape
    rank = basis.shape[0]
    return pl.pallas_call(
        right_kernel,
        grid=(lists,),
        in_specs=[
            pl.BlockSpec((1, slots, width), lambda l: (l, 0, 0)),
            pl.BlockSpec((rank, width), lambda l: (0, 0)),
        ],
        out_specs=pl.BlockSpec((rank + EXTRA, slots), lambda l: (0, l)),
        out_shape=jax.ShapeDtypeStruct((rank + EXTRA, lists * slots), jnp.float32),
        cost_estimate=pl.CostEstimate(flops=8 * lists * slots * width * rank, bytes_accessed=2 * out_grads.size, transcendentals=0),
        compiler_params=pltpu.CompilerParams(vmem_limit_bytes=52 << 20),
        name="project_right",
    )(out_grads, basis)


def left_kernel(first, lists, lengths, acts, basis, out, held, arrived):
    rank = basis.shape[0]
    depth, slots = held.shape[:2]
    pieces = arrived.shape[1]
    rows = slots // pieces
    unit = slots // UNITS

    def each(l, slot, act):
        for piece in range(pieces):
            @pl.when(piece * rows < lengths[first + l])
            def _():
                part = pl.ds(piece * rows, rows)
                act(pltpu.make_async_copy(acts.at[first + l, part, :], held.at[slot, part, :], arrived.at[slot, piece]))

    for l in range(min(depth, lists)):
        each(l, l, lambda copy: copy.start())
    out[...] = jnp.zeros_like(out)

    def step(l, carry):
        slot = lax.rem(l, depth)
        each(l, slot, lambda copy: copy.wait())
        count = lengths[first + l]
        for units in range(1, UNITS + 1):
            @pl.when((count + unit - 1) // unit == units)
            def _():
                size = units * unit
                left = lax.dot_general(held[slot, :size, :], basis[...], NT, preferred_element_type=jnp.float32)
                row = lax.broadcasted_iota(jnp.int32, left.shape, 0)
                left = jnp.where(row < count, left, 0.0)
                head = left.astype(jnp.bfloat16)
                place = pl.ds(pl.multiple_of(l * slots, slots), size)
                out[place, :rank] = head
                out[place, rank:] = (left - head.astype(jnp.float32)).astype(jnp.bfloat16)

        @pl.when(l + depth < lists)
        def _():
            each(l + depth, slot, lambda copy: copy.start())
        return carry

    lax.fori_loop(0, lists, step, 0)


def project_left(activations, basis, lengths, first, lists):
    slots, width = activations.shape[1:]
    rank = basis.shape[0]
    depth, pieces = 3, slots // 64
    return pl.pallas_call(
        functools.partial(left_kernel, first, lists),
        in_specs=[
            pl.BlockSpec(memory_space=pltpu.SMEM),
            pl.BlockSpec(memory_space=pl.ANY),
            pl.BlockSpec(memory_space=pltpu.VMEM),
        ],
        out_specs=pl.BlockSpec(memory_space=pltpu.VMEM),
        out_shape=jax.ShapeDtypeStruct((lists * slots, 2 * rank), jnp.bfloat16),
        scratch_shapes=[pltpu.VMEM((depth, slots, width), activations.dtype), pltpu.SemaphoreType.DMA((depth, pieces))],
        cost_estimate=pl.CostEstimate(flops=8 * lists * slots * width * rank, bytes_accessed=2 * lists * slots * width, transcendentals=0),
        compiler_params=pltpu.CompilerParams(vmem_limit_bytes=32 << 20),
        name="project_left",
    )(lengths, activations, basis)


def sketch_kernel(where, rights, left_a, left_b, out, both, sums):
    lists, rank = sums.shape[:2]
    width = rights.shape[2]
    slots = both.shape[1] // lists
    for block in range(rights.shape[0]):
        value = rights[block]
        head = value.astype(jnp.bfloat16)
        columns = pl.ds(pl.multiple_of(where[block] * width, width), width)
        both[:rank, columns] = head
        both[rank:, columns] = (value - head.astype(jnp.float32)).astype(jnp.bfloat16)
    early = left_a.shape[0] // slots
    for l in range(lists):
        left = left_a[l * slots:(l + 1) * slots] if l < early else left_b[(l - early) * slots:(l - early + 1) * slots]
        full = lax.dot_general(both[:, l * slots:(l + 1) * slots], left, NN, preferred_element_type=jnp.float32)
        side = full[:rank] + full[rank:]
        sums[l] = (side[:, :rank] + side[:, rank:]).T
    rows = out.shape[2] // rank
    for i in range(rank):
        column = (i % rows) * rank
        out[i // rows, :lists, column:column + rank] = sums[:, i, :]


def sketch_terms(where, rights, left_a, left_b, lists, slots, groups):
    rank = rights.shape[1]
    vmem = pl.BlockSpec(memory_space=pltpu.VMEM)
    return pl.pallas_call(
        sketch_kernel,
        in_specs=[pl.BlockSpec(memory_space=pltpu.SMEM), vmem, vmem, vmem],
        out_specs=vmem,
        out_shape=jax.ShapeDtypeStruct((groups, 8, rank * rank // groups), jnp.float32),
        scratch_shapes=[pltpu.VMEM((2 * rank, lists * slots), jnp.bfloat16), pltpu.VMEM((lists, rank, rank), jnp.float32)],
        compiler_params=pltpu.CompilerParams(vmem_limit_bytes=32 << 20),
        name="sketch_terms",
    )(where, rights, left_a, left_b)


def score_kernel(*refs):
    sketches, queries, out = refs[:-2], refs[-2], refs[-1]
    count = queries.shape[0]
    value = jnp.concatenate([s[...] for s in sketches], axis=0)
    head = value.astype(jnp.bfloat16)
    both = jnp.concatenate([head, (value - head.astype(jnp.float32)).astype(jnp.bfloat16)], axis=0)
    full = lax.dot_general(both, queries[...], NT, preferred_element_type=jnp.float32)
    rows = value.shape[0]
    terms = full[:rows] + full[rows:]
    squares = jnp.sum(value * value, axis=1, keepdims=True)
    for group in range(len(sketches)):
        out[group, :, :count] = terms[group * 8:group * 8 + 8]
        out[group, :, count:] = jnp.broadcast_to(squares[group * 8:group * 8 + 8], (8, 128))


def score_terms(sketches, queries):
    vmem = pl.BlockSpec(memory_space=pltpu.VMEM)
    return pl.pallas_call(
        score_kernel,
        in_specs=[vmem] * (len(sketches) + 1),
        out_specs=vmem,
        out_shape=jax.ShapeDtypeStruct((len(sketches), 8, queries.shape[0] + 128), jnp.float32),
        compiler_params=pltpu.CompilerParams(vmem_limit_bytes=40 << 20),
        name="score_terms",
    )(*sketches, queries)


def ring(size, shift):
    return [(i, (i + shift) % size) for i in range(size)]


def decoded(coded, rank):
    wide = coded.astype(jnp.float32)
    return wide[..., :rank, :] * jnp.exp2(wide[..., rank:rank + 1, :] - TOP)


def local_square(activations, out_grads, lengths, proj_in, proj_out, queries):
    lists, slots, _ = activations.shape
    rank = proj_in.shape[1]
    groups = lax.axis_size("tensor")
    me = lax.axis_index("tensor")
    shifts = range(1, groups)
    tokens = lists * slots
    block = tokens // groups

    right = project_right(out_grads, proj_out.T)
    coded = right.astype(jnp.float16)

    def part(shift):
        return lax.dynamic_slice_in_dim(coded, (me + shift) % groups * block, block, 1)

    arrived = [lax.ppermute(part(shift), "tensor", ring(groups, shift)) for shift in shifts]
    early = lists // 2
    left_a = project_left(activations, proj_in.T, lengths, 0, early)
    pieces = [part(0)] + arrived
    wide = [p.astype(jnp.float32) for p in pieces]
    summed = sum(w * jnp.exp2(w[rank:rank + 1] - TOP) for w in wide)
    exponent = functools.reduce(jnp.maximum, [w[rank:rank + 1] for w in wide]) + (groups - 1).bit_length()
    row = lax.broadcasted_iota(jnp.int32, summed.shape, 0)
    mine = jnp.where(row < rank, summed * jnp.exp2(TOP - exponent), exponent).astype(jnp.float16)
    mine, later = lax.optimization_barrier((mine, lengths))
    blocks = [mine] + [lax.ppermute(mine, "tensor", ring(groups, shift)) for shift in shifts]
    left_b = project_left(activations, proj_in.T, later, early, lists - early)
    rights = decoded(jnp.stack(blocks), rank)
    where = (me - jnp.arange(groups, dtype=jnp.int32)) % groups
    terms = sketch_terms(where, rights, left_a, left_b, lists, slots, groups)

    def towards(array, index):
        return lax.dynamic_index_in_dim(array, index, 0, keepdims=False)

    sketch = towards(terms, me)
    for shift in shifts:
        sketch = sketch + lax.ppermute(towards(terms, (me + shift) % groups), "tensor", ring(groups, shift))
    sketches = [sketch] + [lax.ppermute(sketch, "example", ring(groups, shift)) for shift in shifts]
    scores = score_terms(sketches, queries)
    here = lax.axis_index("example")
    final = None
    for shift in range(groups):
        target = (me + shift) % groups
        pairs = [
            (t * groups + e, e * groups + (t + shift) % groups)
            for t in range(groups) for e in range(groups)
        ]
        moved = lax.ppermute(towards(scores, (here - target) % groups), ("tensor", "example"), pairs)
        final = moved if final is None else final + moved
    count = queries.shape[0]
    return final[:lists, :count] * lax.rsqrt(final[:lists, count:count + 1] + 1e-06)


def local(activations, out_grads, lengths, proj_in, proj_out, queries):
    nlists, slots, hidden_width = activations.shape
    feature_width = out_grads.shape[2]
    rank = proj_in.shape[1]
    left_part = jnp.dot(
        activations.reshape(nlists * slots, hidden_width),
        proj_in,
        preferred_element_type=jnp.float32,
    )
    right_part = jnp.dot(
        out_grads.reshape(nlists * slots, feature_width),
        proj_out,
        preferred_element_type=jnp.float32,
    )
    stacked = jnp.concatenate([left_part, right_part], axis=1).reshape(nlists, slots, 2 * rank)
    groups = lax.axis_size("tensor")
    block_rows = rank // groups
    summed = lax.psum(stacked, "tensor")
    positions = lax.broadcasted_iota(jnp.int32, (nlists, slots), 1)
    keep = (positions < lengths[:, None]).astype(jnp.float32)[:, :, None]
    left_full = summed[:, :, :rank] * keep
    right_full = summed[:, :, rank:]
    sketch = jnp.einsum("ltr,lts->lrs", left_full, right_full, precision=lax.Precision.HIGHEST)
    totals = jnp.sum(sketch * sketch, axis=(1, 2))
    unit_all = (sketch / jnp.sqrt(totals + 1e-06)[:, None, None]).astype(jnp.bfloat16)
    first_row = lax.axis_index("tensor") * block_rows
    mine = lax.dynamic_slice_in_dim(unit_all, first_row, block_rows, 1)
    mine = mine.reshape(nlists, block_rows * rank)
    terms = lax.dot_general(
        mine,
        lax.all_gather(queries, "example", axis=0, tiled=True),
        (((1,), (1,)), ((), ())),
        preferred_element_type=jnp.float32,
    )
    return lax.psum_scatter(terms, "tensor", scatter_dimension=1, tiled=True)


def solution(mesh):
    in_specs = (
        P(("parts", "example"), None, "tensor"),
        P(("parts", "example"), None, "tensor"),
        P(("parts", "example")),
        P("tensor", None),
        P("tensor", None),
        P(("parts", "example"), "tensor"),
    )
    out_specs = P(("parts", "example"), "tensor")
    square = mesh.shape["tensor"] == mesh.shape["example"]
    plan = local_square if square else local
    return jax.shard_map(plan, mesh=mesh, in_specs=in_specs, out_specs=out_specs, check_vma=False)
```

```python
import functools

import jax
import jax.numpy as jnp
from jax import lax
from jax.experimental import pallas as pl
from jax.experimental.pallas import tpu as pltpu
from jax.sharding import PartitionSpec as P

TOP = 14.0
EXTRA = 8
LANES = 128
UNITS = 4
NT = (((1,), (1,)), ((), ()))
NN = (((1,), (0,)), ((), ()))


def leveled(value):
    largest = jnp.max(jnp.abs(value), axis=1, keepdims=True)
    exponent = jnp.ceil(jnp.log2(jnp.maximum(largest, 1e-30)))
    return value * jnp.exp2(TOP - exponent), exponent


def right_kernel(grads, basis, out, held, weights, arrived):
    rank = basis.shape[0]
    lists, slots = held.shape[:2]
    load = pltpu.make_async_copy(basis, weights, arrived.at[lists])
    load.start()

    def copy(l):
        return pltpu.make_async_copy(grads.at[l], held.at[l], arrived.at[l])

    for l in range(lists):
        copy(l).start()
    load.wait()

    def step(l, carry):
        copy(l).wait()
        right = lax.dot_general(held[l], weights[...], NT, preferred_element_type=jnp.float32).T
        largest = jnp.max(jnp.abs(right), axis=0, keepdims=True)
        exponent = jnp.ceil(jnp.log2(jnp.maximum(largest, 1e-30)))
        columns = pl.ds(pl.multiple_of(l * slots, slots), slots)
        out[:rank, columns] = right * jnp.exp2(TOP - exponent)
        out[rank:, columns] = jnp.broadcast_to(exponent, (EXTRA, slots))
        return carry

    lax.fori_loop(0, lists, step, 0)


def project_right(out_grads, basis):
    slots, width = out_grads.shape[1:]
    rank = basis.shape[0]
    tokens = out_grads.shape[0] * slots
    pieces = out_grads.reshape(tokens // slots, slots, width)
    return pl.pallas_call(
        right_kernel,
        in_specs=[pl.BlockSpec(memory_space=pl.ANY)] * 2,
        out_specs=pl.BlockSpec(memory_space=pltpu.VMEM),
        out_shape=jax.ShapeDtypeStruct((rank + EXTRA, tokens), jnp.float32),
        scratch_shapes=[
            pltpu.VMEM(pieces.shape, out_grads.dtype),
            pltpu.VMEM(basis.shape, basis.dtype),
            pltpu.SemaphoreType.DMA((pieces.shape[0] + 1,)),
        ],
        cost_estimate=pl.CostEstimate(flops=8 * tokens * width * rank, bytes_accessed=2 * out_grads.size, transcendentals=0),
        compiler_params=pltpu.CompilerParams(vmem_limit_bytes=52 << 20),
        name="project_right",
    )(pieces, basis)


def left_kernel(first, slots, lengths, acts, basis, out, held, arrived):
    rank = basis.shape[0]
    depth, size = held.shape[:2]
    pieces = arrived.shape[1]
    rows, unit = size // pieces, size // UNITS
    steps = out.shape[0] // size
    cuts = slots // size

    def count_of(n):
        return lengths[first + n // cuts] - n % cuts * size

    def each(n, slot, act):
        count = count_of(n)
        for piece in range(pieces):
            @pl.when(piece * rows < count)
            def _():
                source = pl.ds(pl.multiple_of(n % cuts * size + piece * rows, rows), rows)
                act(pltpu.make_async_copy(acts.at[first + n // cuts, source, :], held.at[slot, pl.ds(piece * rows, rows), :], arrived.at[slot, piece]))

    for n in range(min(depth, steps)):
        each(n, n, lambda copy: copy.start())
    out[...] = jnp.zeros_like(out)

    def step(n, carry):
        slot = lax.rem(n, depth)
        each(n, slot, lambda copy: copy.wait())
        count = count_of(n)
        needed = jnp.minimum((count + unit - 1) // unit, UNITS)
        for units in range(1, UNITS + 1):
            @pl.when(needed == units)
            def _():
                left = lax.dot_general(held[slot, :units * unit, :], basis[...], NT, preferred_element_type=jnp.float32)
                row = lax.broadcasted_iota(jnp.int32, left.shape, 0)
                left = jnp.where(row < count, left, 0.0)
                head = left.astype(jnp.bfloat16)
                place = pl.ds(pl.multiple_of(n * size, size), units * unit)
                out[place, :rank] = head
                out[place, rank:] = (left - head.astype(jnp.float32)).astype(jnp.bfloat16)

        @pl.when(n + depth < steps)
        def _():
            each(n + depth, slot, lambda copy: copy.start())
        return carry

    lax.fori_loop(0, steps, step, 0)


def project_left(activations, basis, lengths, first, lists):
    slots, width = activations.shape[1:]
    rank = basis.shape[0]
    size, depth = 256, 6
    return pl.pallas_call(
        functools.partial(left_kernel, first, slots),
        in_specs=[
            pl.BlockSpec(memory_space=pltpu.SMEM),
            pl.BlockSpec(memory_space=pl.ANY),
            pl.BlockSpec(memory_space=pltpu.VMEM),
        ],
        out_specs=pl.BlockSpec(memory_space=pltpu.VMEM),
        out_shape=jax.ShapeDtypeStruct((lists * slots, 2 * rank), jnp.bfloat16),
        scratch_shapes=[pltpu.VMEM((depth, size, width), activations.dtype), pltpu.SemaphoreType.DMA((depth, size // 64))],
        cost_estimate=pl.CostEstimate(flops=8 * lists * slots * width * rank, bytes_accessed=2 * lists * slots * width, transcendentals=0),
        compiler_params=pltpu.CompilerParams(vmem_limit_bytes=36 << 20),
        name="project_left",
    )(lengths, activations, basis)


def sketch_kernel(where, rights, left_a, left_b, out, both, sums):
    out[...] = jnp.zeros_like(out)
    lists, rank = sums.shape[:2]
    width = rights.shape[2]
    slots = both.shape[1] // lists
    for block in range(rights.shape[0]):
        value = rights[block]
        head = value.astype(jnp.bfloat16)
        columns = pl.ds(pl.multiple_of(where[block] * width, width), width)
        both[:rank, columns] = head
        both[rank:, columns] = (value - head.astype(jnp.float32)).astype(jnp.bfloat16)
    early = left_a.shape[0] // slots
    for l in range(lists):
        left = left_a[l * slots:(l + 1) * slots] if l < early else left_b[(l - early) * slots:(l - early + 1) * slots]
        full = lax.dot_general(both[:, l * slots:(l + 1) * slots], left, NN, preferred_element_type=jnp.float32)
        side = full[:rank] + full[rank:]
        sums[l] = (side[:, :rank] + side[:, rank:]).T
    rows = rank // out.shape[0]
    for i in range(rank):
        column = (i % rows) * rank
        out[i // rows, :lists, column:column + rank] = sums[:, i, :]
    for group in range(out.shape[0]):
        scaled, exponent = leveled(out[group, :lists, :rows * rank])
        out[group, :lists, :rows * rank] = scaled
        out[group, :lists, rows * rank:] = jnp.broadcast_to(exponent, (lists, LANES))


def sketch_terms(where, rights, left_a, left_b, lists, slots, groups):
    rank = rights.shape[1]
    vmem = pl.BlockSpec(memory_space=pltpu.VMEM)
    return pl.pallas_call(
        sketch_kernel,
        in_specs=[pl.BlockSpec(memory_space=pltpu.SMEM), vmem, vmem, vmem],
        out_specs=vmem,
        out_shape=jax.ShapeDtypeStruct((groups, 8, rank * rank // groups + LANES), jnp.float32),
        scratch_shapes=[pltpu.VMEM((2 * rank, lists * slots), jnp.bfloat16), pltpu.VMEM((lists, rank, rank), jnp.float32)],
        compiler_params=pltpu.CompilerParams(vmem_limit_bytes=32 << 20),
        name="sketch_terms",
    )(where, rights, left_a, left_b)


def score_kernel(*refs):
    sketches, queries, out = refs[:-2], refs[-2], refs[-1]
    count = queries.shape[0]
    value = jnp.concatenate([s[...] for s in sketches], axis=0)
    head = value.astype(jnp.bfloat16)
    both = jnp.concatenate([head, (value - head.astype(jnp.float32)).astype(jnp.bfloat16)], axis=0)
    full = lax.dot_general(both, queries[...], NT, preferred_element_type=jnp.float32)
    rows = value.shape[0]
    terms = full[:rows] + full[rows:]
    squares = jnp.sum(value * value, axis=1, keepdims=True)
    scaled, exponent = leveled(terms)
    square, power = leveled(squares)
    lane = lax.broadcasted_iota(jnp.int32, (rows, LANES), 1)
    notes = jnp.where(lane == 0, exponent, jnp.where(lane == 1, square, power))
    for group in range(len(sketches)):
        out[group, :, :count] = scaled[group * 8:group * 8 + 8]
        out[group, :, count:] = notes[group * 8:group * 8 + 8]


def score_terms(sketches, queries):
    vmem = pl.BlockSpec(memory_space=pltpu.VMEM)
    return pl.pallas_call(
        score_kernel,
        in_specs=[vmem] * (len(sketches) + 1),
        out_specs=vmem,
        out_shape=jax.ShapeDtypeStruct((len(sketches), 8, queries.shape[0] + LANES), jnp.float32),
        compiler_params=pltpu.CompilerParams(vmem_limit_bytes=40 << 20),
        name="score_terms",
    )(*sketches, queries)


def ring(size, shift):
    return [(i, (i + shift) % size) for i in range(size)]


def decoded(coded, rank):
    wide = coded.astype(jnp.float32)
    return wide[..., :rank, :] * jnp.exp2(wide[..., rank:rank + 1, :] - TOP)


def local_square(activations, out_grads, lengths, proj_in, proj_out, queries):
    lists, slots, _ = activations.shape
    rank = proj_in.shape[1]
    groups = lax.axis_size("tensor")
    me = lax.axis_index("tensor")
    shifts = range(1, groups)
    tokens = lists * slots
    block = tokens // groups

    right = project_right(out_grads, proj_out.T)
    coded = right.astype(jnp.float16)

    def part(shift):
        return lax.dynamic_slice_in_dim(coded, (me + shift) % groups * block, block, 1)

    arrived = [lax.ppermute(part(shift), "tensor", ring(groups, shift)) for shift in shifts]
    early = lists // 2
    left_a = project_left(activations, proj_in.T, lengths, 0, early)
    pieces = [part(0)] + arrived
    wide = [p.astype(jnp.float32) for p in pieces]
    summed = sum(w * jnp.exp2(w[rank:rank + 1] - TOP) for w in wide)
    exponent = functools.reduce(jnp.maximum, [w[rank:rank + 1] for w in wide]) + (groups - 1).bit_length()
    row = lax.broadcasted_iota(jnp.int32, summed.shape, 0)
    mine = jnp.where(row < rank, summed * jnp.exp2(TOP - exponent), exponent).astype(jnp.float16)
    mine, later = lax.optimization_barrier((mine, lengths))
    blocks = [mine] + [lax.ppermute(mine, "tensor", ring(groups, shift)) for shift in shifts]
    left_b = project_left(activations, proj_in.T, later, early, lists - early)
    rights = decoded(jnp.stack(blocks), rank)
    where = (me - jnp.arange(groups, dtype=jnp.int32)) % groups
    terms = sketch_terms(where, rights, left_a, left_b, lists, slots, groups)

    def towards(array, index):
        return lax.dynamic_index_in_dim(array, index, 0, keepdims=False)

    coded = terms.astype(jnp.float16)
    entries = rank * rank // groups
    sketch = None
    for shift in range(groups):
        piece = towards(coded, (me + shift) % groups)
        if shift:
            piece = lax.ppermute(piece, "tensor", ring(groups, shift))
        piece = piece.astype(jnp.float32)
        piece = piece[:, :entries] * jnp.exp2(piece[:, entries:entries + 1] - TOP)
        sketch = piece if sketch is None else sketch + piece
    sketches = [sketch] + [lax.ppermute(sketch, "example", ring(groups, shift)) for shift in shifts]
    scores = score_terms(sketches, queries).astype(jnp.float16)
    count = queries.shape[0]
    here = lax.axis_index("example")
    final, square = 0.0, 0.0
    for shift in range(groups):
        target = (me + shift) % groups
        pairs = [
            (t * groups + e, e * groups + (t + shift) % groups)
            for t in range(groups) for e in range(groups)
        ]
        moved = lax.ppermute(towards(scores, (here - target) % groups), ("tensor", "example"), pairs).astype(jnp.float32)
        final += moved[:lists, :count] * jnp.exp2(moved[:lists, count:count + 1] - TOP)
        square += moved[:lists, count + 1:count + 2] * jnp.exp2(moved[:lists, count + 2:count + 3] - TOP)
    return final * lax.rsqrt(square + 1e-06)


def local(activations, out_grads, lengths, proj_in, proj_out, queries):
    nlists, slots, hidden_width = activations.shape
    feature_width = out_grads.shape[2]
    rank = proj_in.shape[1]
    left_part = jnp.dot(
        activations.reshape(nlists * slots, hidden_width),
        proj_in,
        preferred_element_type=jnp.float32,
    )
    right_part = jnp.dot(
        out_grads.reshape(nlists * slots, feature_width),
        proj_out,
        preferred_element_type=jnp.float32,
    )
    stacked = jnp.concatenate([left_part, right_part], axis=1).reshape(nlists, slots, 2 * rank)
    groups = lax.axis_size("tensor")
    block_rows = rank // groups
    summed = lax.psum(stacked, "tensor")
    positions = lax.broadcasted_iota(jnp.int32, (nlists, slots), 1)
    keep = (positions < lengths[:, None]).astype(jnp.float32)[:, :, None]
    left_full = summed[:, :, :rank] * keep
    right_full = summed[:, :, rank:]
    sketch = jnp.einsum("ltr,lts->lrs", left_full, right_full, precision=lax.Precision.HIGHEST)
    totals = jnp.sum(sketch * sketch, axis=(1, 2))
    unit_all = (sketch / jnp.sqrt(totals + 1e-06)[:, None, None]).astype(jnp.bfloat16)
    first_row = lax.axis_index("tensor") * block_rows
    mine = lax.dynamic_slice_in_dim(unit_all, first_row, block_rows, 1)
    mine = mine.reshape(nlists, block_rows * rank)
    terms = lax.dot_general(
        mine,
        lax.all_gather(queries, "example", axis=0, tiled=True),
        (((1,), (1,)), ((), ())),
        preferred_element_type=jnp.float32,
    )
    return lax.psum_scatter(terms, "tensor", scatter_dimension=1, tiled=True)


def solution(mesh):
    in_specs = (
        P(("parts", "example"), None, "tensor"),
        P(("parts", "example"), None, "tensor"),
        P(("parts", "example")),
        P("tensor", None),
        P("tensor", None),
        P(("parts", "example"), "tensor"),
    )
    out_specs = P(("parts", "example"), "tensor")
    square = mesh.shape["tensor"] == mesh.shape["example"]
    plan = local_square if square else local
    return jax.shard_map(plan, mesh=mesh, in_specs=in_specs, out_specs=out_specs, check_vma=False)
```

```python
import functools

import jax
import jax.numpy as jnp
from jax import lax
from jax.experimental import pallas as pl
from jax.experimental.pallas import tpu as pltpu
from jax.sharding import PartitionSpec as P

TOP = 14.0
EXTRA = 8
LANES = 128
UNITS = 4
NT = (((1,), (1,)), ((), ()))
NN = (((1,), (0,)), ((), ()))


def leveled(value):
    largest = jnp.max(jnp.abs(value), axis=1, keepdims=True)
    exponent = jnp.ceil(jnp.log2(jnp.maximum(largest, 1e-30)))
    return value * jnp.exp2(TOP - exponent), exponent


def right_kernel(grads, basis, out, held, weights, arrived):
    rank = basis.shape[0]
    lists, slots = held.shape[:2]
    load = pltpu.make_async_copy(basis, weights, arrived.at[lists])
    load.start()

    def copy(l):
        return pltpu.make_async_copy(grads.at[l], held.at[l], arrived.at[l])

    for l in range(lists):
        copy(l).start()
    load.wait()

    def step(l, carry):
        copy(l).wait()
        right = lax.dot_general(held[l], weights[...], NT, preferred_element_type=jnp.float32).T
        largest = jnp.max(jnp.abs(right), axis=0, keepdims=True)
        exponent = jnp.ceil(jnp.log2(jnp.maximum(largest, 1e-30)))
        columns = pl.ds(pl.multiple_of(l * slots, slots), slots)
        out[:rank, columns] = right * jnp.exp2(TOP - exponent)
        out[rank:, columns] = jnp.broadcast_to(exponent, (EXTRA, slots))
        return carry

    lax.fori_loop(0, lists, step, 0)


def project_right(out_grads, basis):
    slots, width = out_grads.shape[1:]
    rank = basis.shape[0]
    tokens = out_grads.shape[0] * slots
    pieces = out_grads.reshape(tokens // slots, slots, width)
    return pl.pallas_call(
        right_kernel,
        in_specs=[pl.BlockSpec(memory_space=pltpu.HBM)] * 2,
        out_specs=pl.BlockSpec(memory_space=pltpu.VMEM),
        out_shape=jax.ShapeDtypeStruct((rank + EXTRA, tokens), jnp.float32),
        scratch_shapes=[
            pltpu.VMEM(pieces.shape, out_grads.dtype),
            pltpu.VMEM(basis.shape, basis.dtype),
            pltpu.SemaphoreType.DMA((pieces.shape[0] + 1,)),
        ],
        cost_estimate=pl.CostEstimate(flops=8 * tokens * width * rank, bytes_accessed=2 * out_grads.size, transcendentals=0),
        compiler_params=pltpu.CompilerParams(vmem_limit_bytes=52 << 20),
        name="project_right",
    )(pieces, pltpu.with_memory_space_constraint(basis, pltpu.HBM))


def left_kernel(first, slots, lengths, acts, basis, out, held, arrived):
    rank = basis.shape[0]
    depth, size = held.shape[:2]
    pieces = arrived.shape[1]
    rows, unit = size // pieces, size // UNITS
    steps = out.shape[0] // size
    cuts = slots // size

    def count_of(n):
        return lengths[first + n // cuts] - n % cuts * size

    def each(n, slot, act):
        count = count_of(n)
        for piece in range(pieces):
            @pl.when(piece * rows < count)
            def _():
                source = pl.ds(pl.multiple_of(n % cuts * size + piece * rows, rows), rows)
                act(pltpu.make_async_copy(acts.at[first + n // cuts, source, :], held.at[slot, pl.ds(piece * rows, rows), :], arrived.at[slot, piece]))

    for n in range(min(depth, steps)):
        each(n, n, lambda copy: copy.start())
    out[...] = jnp.zeros_like(out)

    def step(n, carry):
        slot = lax.rem(n, depth)
        each(n, slot, lambda copy: copy.wait())
        count = count_of(n)
        needed = jnp.minimum((count + unit - 1) // unit, UNITS)
        for units in range(1, UNITS + 1):
            @pl.when(needed == units)
            def _():
                left = lax.dot_general(held[slot, :units * unit, :], basis[...], NT, preferred_element_type=jnp.float32)
                row = lax.broadcasted_iota(jnp.int32, left.shape, 0)
                left = jnp.where(row < count, left, 0.0)
                head = left.astype(jnp.bfloat16)
                place = pl.ds(pl.multiple_of(n * size, size), units * unit)
                out[place, :rank] = head
                out[place, rank:] = (left - head.astype(jnp.float32)).astype(jnp.bfloat16)

        @pl.when(n + depth < steps)
        def _():
            each(n + depth, slot, lambda copy: copy.start())
        return carry

    lax.fori_loop(0, steps, step, 0)


def project_left(activations, basis, lengths, first, lists):
    slots, width = activations.shape[1:]
    rank = basis.shape[0]
    size, depth = 256, 6
    return pl.pallas_call(
        functools.partial(left_kernel, first, slots),
        in_specs=[
            pl.BlockSpec(memory_space=pltpu.SMEM),
            pl.BlockSpec(memory_space=pl.ANY),
            pl.BlockSpec(memory_space=pltpu.VMEM),
        ],
        out_specs=pl.BlockSpec(memory_space=pltpu.VMEM),
        out_shape=jax.ShapeDtypeStruct((lists * slots, 2 * rank), jnp.bfloat16),
        scratch_shapes=[pltpu.VMEM((depth, size, width), activations.dtype), pltpu.SemaphoreType.DMA((depth, size // 64))],
        cost_estimate=pl.CostEstimate(flops=8 * lists * slots * width * rank, bytes_accessed=2 * lists * slots * width, transcendentals=0),
        compiler_params=pltpu.CompilerParams(vmem_limit_bytes=36 << 20),
        name="project_left",
    )(lengths, activations, basis)


def sketch_kernel(where, rights, left_a, left_b, out, both, sums):
    out[...] = jnp.zeros_like(out)
    lists, rank = sums.shape[:2]
    width = rights.shape[2]
    slots = both.shape[1] // lists
    for block in range(rights.shape[0]):
        value = rights[block]
        head = value.astype(jnp.bfloat16)
        columns = pl.ds(pl.multiple_of(where[block] * width, width), width)
        both[:rank, columns] = head
        both[rank:, columns] = (value - head.astype(jnp.float32)).astype(jnp.bfloat16)
    early = left_a.shape[0] // slots
    for l in range(lists):
        left = left_a[l * slots:(l + 1) * slots] if l < early else left_b[(l - early) * slots:(l - early + 1) * slots]
        full = lax.dot_general(both[:, l * slots:(l + 1) * slots], left, NN, preferred_element_type=jnp.float32)
        side = full[:rank] + full[rank:]
        sums[l] = (side[:, :rank] + side[:, rank:]).T
    rows = rank // out.shape[0]
    for i in range(rank):
        column = (i % rows) * rank
        out[i // rows, :lists, column:column + rank] = sums[:, i, :]
    for group in range(out.shape[0]):
        scaled, exponent = leveled(out[group, :lists, :rows * rank])
        out[group, :lists, :rows * rank] = scaled
        out[group, :lists, rows * rank:] = jnp.broadcast_to(exponent, (lists, LANES))


def sketch_terms(where, rights, left_a, left_b, lists, slots, groups):
    rank = rights.shape[1]
    vmem = pl.BlockSpec(memory_space=pltpu.VMEM)
    return pl.pallas_call(
        sketch_kernel,
        in_specs=[pl.BlockSpec(memory_space=pltpu.SMEM), vmem, vmem, vmem],
        out_specs=vmem,
        out_shape=jax.ShapeDtypeStruct((groups, 8, rank * rank // groups + LANES), jnp.float32),
        scratch_shapes=[pltpu.VMEM((2 * rank, lists * slots), jnp.bfloat16), pltpu.VMEM((lists, rank, rank), jnp.float32)],
        compiler_params=pltpu.CompilerParams(vmem_limit_bytes=32 << 20),
        name="sketch_terms",
    )(where, rights, left_a, left_b)


def score_kernel(*refs):
    sketches, queries, out = refs[:-2], refs[-2], refs[-1]
    count = queries.shape[0]
    value = jnp.concatenate([s[...] for s in sketches], axis=0)
    head = value.astype(jnp.bfloat16)
    both = jnp.concatenate([head, (value - head.astype(jnp.float32)).astype(jnp.bfloat16)], axis=0)
    full = lax.dot_general(both, queries[...], NT, preferred_element_type=jnp.float32)
    rows = value.shape[0]
    terms = full[:rows] + full[rows:]
    squares = jnp.sum(value * value, axis=1, keepdims=True)
    scaled, exponent = leveled(terms)
    square, power = leveled(squares)
    lane = lax.broadcasted_iota(jnp.int32, (rows, LANES), 1)
    notes = jnp.where(lane == 0, exponent, jnp.where(lane == 1, square, power))
    for group in range(len(sketches)):
        out[group, :, :count] = scaled[group * 8:group * 8 + 8]
        out[group, :, count:] = notes[group * 8:group * 8 + 8]


def score_terms(sketches, queries):
    vmem = pl.BlockSpec(memory_space=pltpu.VMEM)
    return pl.pallas_call(
        score_kernel,
        in_specs=[vmem] * (len(sketches) + 1),
        out_specs=vmem,
        out_shape=jax.ShapeDtypeStruct((len(sketches), 8, queries.shape[0] + LANES), jnp.float32),
        compiler_params=pltpu.CompilerParams(vmem_limit_bytes=40 << 20),
        name="score_terms",
    )(*sketches, queries)


def ring(size, shift):
    return [(i, (i + shift) % size) for i in range(size)]


def decoded(coded, rank):
    wide = coded.astype(jnp.float32)
    return wide[..., :rank, :] * jnp.exp2(wide[..., rank:rank + 1, :] - TOP)


def local_square(activations, out_grads, lengths, proj_in, proj_out, queries):
    lists, slots, _ = activations.shape
    rank = proj_in.shape[1]
    groups = lax.axis_size("tensor")
    me = lax.axis_index("tensor")
    shifts = range(1, groups)
    tokens = lists * slots
    block = tokens // groups

    right = project_right(out_grads, proj_out.T)
    coded = right.astype(jnp.float16)

    def part(shift):
        return lax.dynamic_slice_in_dim(coded, (me + shift) % groups * block, block, 1)

    arrived = [lax.ppermute(part(shift), "tensor", ring(groups, shift)) for shift in shifts]
    early = lists // 2
    left_a = project_left(activations, proj_in.T, lengths, 0, early)
    pieces = [part(0)] + arrived
    wide = [p.astype(jnp.float32) for p in pieces]
    summed = sum(w * jnp.exp2(w[rank:rank + 1] - TOP) for w in wide)
    exponent = functools.reduce(jnp.maximum, [w[rank:rank + 1] for w in wide]) + (groups - 1).bit_length()
    row = lax.broadcasted_iota(jnp.int32, summed.shape, 0)
    mine = jnp.where(row < rank, summed * jnp.exp2(TOP - exponent), exponent).astype(jnp.float16)
    mine, later = lax.optimization_barrier((mine, lengths))
    blocks = [mine] + [lax.ppermute(mine, "tensor", ring(groups, shift)) for shift in shifts]
    left_b = project_left(activations, proj_in.T, later, early, lists - early)
    rights = decoded(jnp.stack(blocks), rank)
    where = (me - jnp.arange(groups, dtype=jnp.int32)) % groups
    terms = sketch_terms(where, rights, left_a, left_b, lists, slots, groups)

    def towards(array, index):
        return lax.dynamic_index_in_dim(array, index, 0, keepdims=False)

    coded = terms.astype(jnp.float16)
    entries = rank * rank // groups
    sketch = None
    for shift in range(groups):
        piece = towards(coded, (me + shift) % groups)
        if shift:
            piece = lax.ppermute(piece, "tensor", ring(groups, shift))
        piece = piece.astype(jnp.float32)
        piece = piece[:, :entries] * jnp.exp2(piece[:, entries:entries + 1] - TOP)
        sketch = piece if sketch is None else sketch + piece
    sketches = [sketch] + [lax.ppermute(sketch, "example", ring(groups, shift)) for shift in shifts]
    scores = score_terms(sketches, queries).astype(jnp.float16)
    count = queries.shape[0]
    here = lax.axis_index("example")
    final, square = 0.0, 0.0
    for shift in range(groups):
        target = (me + shift) % groups
        pairs = [
            (t * groups + e, e * groups + (t + shift) % groups)
            for t in range(groups) for e in range(groups)
        ]
        moved = lax.ppermute(towards(scores, (here - target) % groups), ("tensor", "example"), pairs).astype(jnp.float32)
        final += moved[:lists, :count] * jnp.exp2(moved[:lists, count:count + 1] - TOP)
        square += moved[:lists, count + 1:count + 2] * jnp.exp2(moved[:lists, count + 2:count + 3] - TOP)
    return final * lax.rsqrt(square + 1e-06)


def local(activations, out_grads, lengths, proj_in, proj_out, queries):
    nlists, slots, hidden_width = activations.shape
    feature_width = out_grads.shape[2]
    rank = proj_in.shape[1]
    left_part = jnp.dot(
        activations.reshape(nlists * slots, hidden_width),
        proj_in,
        preferred_element_type=jnp.float32,
    )
    right_part = jnp.dot(
        out_grads.reshape(nlists * slots, feature_width),
        proj_out,
        preferred_element_type=jnp.float32,
    )
    stacked = jnp.concatenate([left_part, right_part], axis=1).reshape(nlists, slots, 2 * rank)
    groups = lax.axis_size("tensor")
    block_rows = rank // groups
    summed = lax.psum(stacked, "tensor")
    positions = lax.broadcasted_iota(jnp.int32, (nlists, slots), 1)
    keep = (positions < lengths[:, None]).astype(jnp.float32)[:, :, None]
    left_full = summed[:, :, :rank] * keep
    right_full = summed[:, :, rank:]
    sketch = jnp.einsum("ltr,lts->lrs", left_full, right_full, precision=lax.Precision.HIGHEST)
    totals = jnp.sum(sketch * sketch, axis=(1, 2))
    unit_all = (sketch / jnp.sqrt(totals + 1e-06)[:, None, None]).astype(jnp.bfloat16)
    first_row = lax.axis_index("tensor") * block_rows
    mine = lax.dynamic_slice_in_dim(unit_all, first_row, block_rows, 1)
    mine = mine.reshape(nlists, block_rows * rank)
    terms = lax.dot_general(
        mine,
        lax.all_gather(queries, "example", axis=0, tiled=True),
        (((1,), (1,)), ((), ())),
        preferred_element_type=jnp.float32,
    )
    return lax.psum_scatter(terms, "tensor", scatter_dimension=1, tiled=True)


def solution(mesh):
    in_specs = (
        P(("parts", "example"), None, "tensor"),
        P(("parts", "example"), None, "tensor"),
        P(("parts", "example")),
        P("tensor", None),
        P("tensor", None),
        P(("parts", "example"), "tensor"),
    )
    out_specs = P(("parts", "example"), "tensor")
    square = mesh.shape["tensor"] == mesh.shape["example"]
    plan = local_square if square else local
    return jax.shard_map(plan, mesh=mesh, in_specs=in_specs, out_specs=out_specs, check_vma=False)
```

```python
import functools

import jax
import jax.numpy as jnp
from jax import lax
from jax.experimental import pallas as pl
from jax.experimental.pallas import tpu as pltpu
from jax.sharding import PartitionSpec as P

TOP = 14.0
EXTRA = 8
AHEAD = 3
LANES = 128
UNITS = 4
NT = (((1,), (1,)), ((), ()))
NN = (((1,), (0,)), ((), ()))


def leveled(value):
    largest = jnp.max(jnp.abs(value), axis=1, keepdims=True)
    exponent = jnp.ceil(jnp.log2(jnp.maximum(largest, 1e-30)))
    return value * jnp.exp2(TOP - exponent), exponent


def right_kernel(grads, basis, out, held, weights, arrived):
    rank = basis.shape[0]
    lists, slots = held.shape[:2]
    load = pltpu.make_async_copy(basis, weights, arrived.at[lists])
    load.start()

    def copy(l):
        return pltpu.make_async_copy(grads.at[l], held.at[l], arrived.at[l])

    for l in range(min(AHEAD, lists)):
        copy(l).start()
    load.wait()

    def step(l, carry):
        copy(l).wait()

        @pl.when(l + AHEAD < lists)
        def _():
            copy(l + AHEAD).start()

        right = lax.dot_general(held[l], weights[...], NT, preferred_element_type=jnp.float32).T
        largest = jnp.max(jnp.abs(right), axis=0, keepdims=True)
        exponent = jnp.ceil(jnp.log2(jnp.maximum(largest, 1e-30)))
        columns = pl.ds(pl.multiple_of(l * slots, slots), slots)
        out[:rank, columns] = right * jnp.exp2(TOP - exponent)
        out[rank:, columns] = jnp.broadcast_to(exponent, (EXTRA, slots))
        return carry

    lax.fori_loop(0, lists, step, 0)


def project_right(out_grads, basis):
    slots, width = out_grads.shape[1:]
    rank = basis.shape[0]
    tokens = out_grads.shape[0] * slots
    pieces = out_grads.reshape(tokens // slots, slots, width)
    return pl.pallas_call(
        right_kernel,
        in_specs=[pl.BlockSpec(memory_space=pltpu.HBM)] * 2,
        out_specs=pl.BlockSpec(memory_space=pltpu.VMEM),
        out_shape=jax.ShapeDtypeStruct((rank + EXTRA, tokens), jnp.float32),
        scratch_shapes=[
            pltpu.VMEM(pieces.shape, out_grads.dtype),
            pltpu.VMEM(basis.shape, basis.dtype),
            pltpu.SemaphoreType.DMA((pieces.shape[0] + 1,)),
        ],
        cost_estimate=pl.CostEstimate(flops=8 * tokens * width * rank, bytes_accessed=2 * out_grads.size, transcendentals=0),
        compiler_params=pltpu.CompilerParams(vmem_limit_bytes=52 << 20),
        name="project_right",
    )(pieces, pltpu.with_memory_space_constraint(basis, pltpu.HBM))


def left_kernel(first, slots, lengths, acts, basis, out, held, arrived):
    rank = basis.shape[0]
    depth, size = held.shape[:2]
    pieces = arrived.shape[1]
    rows, unit = size // pieces, size // UNITS
    steps = out.shape[0] // size
    cuts = slots // size

    def count_of(n):
        return lengths[first + n // cuts] - n % cuts * size

    def each(n, slot, act):
        count = count_of(n)
        for piece in range(pieces):
            @pl.when(piece * rows < count)
            def _():
                source = pl.ds(pl.multiple_of(n % cuts * size + piece * rows, rows), rows)
                act(pltpu.make_async_copy(acts.at[first + n // cuts, source, :], held.at[slot, pl.ds(piece * rows, rows), :], arrived.at[slot, piece]))

    for n in range(min(depth, steps)):
        each(n, n, lambda copy: copy.start())
    out[...] = jnp.zeros_like(out)

    def step(n, carry):
        slot = lax.rem(n, depth)
        each(n, slot, lambda copy: copy.wait())
        count = count_of(n)
        needed = jnp.minimum((count + unit - 1) // unit, UNITS)
        for units in range(1, UNITS + 1):
            @pl.when(needed == units)
            def _():
                left = lax.dot_general(held[slot, :units * unit, :], basis[...], NT, preferred_element_type=jnp.float32)
                row = lax.broadcasted_iota(jnp.int32, left.shape, 0)
                left = jnp.where(row < count, left, 0.0)
                head = left.astype(jnp.bfloat16)
                place = pl.ds(pl.multiple_of(n * size, size), units * unit)
                out[place, :rank] = head
                out[place, rank:] = (left - head.astype(jnp.float32)).astype(jnp.bfloat16)

        @pl.when(n + depth < steps)
        def _():
            each(n + depth, slot, lambda copy: copy.start())
        return carry

    lax.fori_loop(0, steps, step, 0)


def project_left(activations, basis, lengths, first, lists):
    slots, width = activations.shape[1:]
    rank = basis.shape[0]
    size, depth = 256, 4
    return pl.pallas_call(
        functools.partial(left_kernel, first, slots),
        in_specs=[
            pl.BlockSpec(memory_space=pltpu.SMEM),
            pl.BlockSpec(memory_space=pl.ANY),
            pl.BlockSpec(memory_space=pltpu.VMEM),
        ],
        out_specs=pl.BlockSpec(memory_space=pltpu.VMEM),
        out_shape=jax.ShapeDtypeStruct((lists * slots, 2 * rank), jnp.bfloat16),
        scratch_shapes=[pltpu.VMEM((depth, size, width), activations.dtype), pltpu.SemaphoreType.DMA((depth, size // 64))],
        cost_estimate=pl.CostEstimate(flops=8 * lists * slots * width * rank, bytes_accessed=2 * lists * slots * width, transcendentals=0),
        compiler_params=pltpu.CompilerParams(vmem_limit_bytes=36 << 20),
        name="project_left",
    )(lengths, activations, basis)


def sketch_kernel(where, rights, left_a, left_b, out, both, sums):
    out[...] = jnp.zeros_like(out)
    lists, rank = sums.shape[:2]
    width = rights.shape[2]
    slots = both.shape[1] // lists
    for block in range(rights.shape[0]):
        value = rights[block]
        head = value.astype(jnp.bfloat16)
        columns = pl.ds(pl.multiple_of(where[block] * width, width), width)
        both[:rank, columns] = head
        both[rank:, columns] = (value - head.astype(jnp.float32)).astype(jnp.bfloat16)
    early = left_a.shape[0] // slots
    for l in range(lists):
        left = left_a[l * slots:(l + 1) * slots] if l < early else left_b[(l - early) * slots:(l - early + 1) * slots]
        full = lax.dot_general(both[:, l * slots:(l + 1) * slots], left, NN, preferred_element_type=jnp.float32)
        side = full[:rank] + full[rank:]
        sums[l] = (side[:, :rank] + side[:, rank:]).T
    rows = rank // out.shape[0]
    for i in range(rank):
        column = (i % rows) * rank
        out[i // rows, :lists, column:column + rank] = sums[:, i, :]
    for group in range(out.shape[0]):
        scaled, exponent = leveled(out[group, :lists, :rows * rank])
        out[group, :lists, :rows * rank] = scaled
        out[group, :lists, rows * rank:] = jnp.broadcast_to(exponent, (lists, LANES))


def sketch_terms(where, rights, left_a, left_b, lists, slots, groups):
    rank = rights.shape[1]
    vmem = pl.BlockSpec(memory_space=pltpu.VMEM)
    return pl.pallas_call(
        sketch_kernel,
        in_specs=[pl.BlockSpec(memory_space=pltpu.SMEM), vmem, vmem, vmem],
        out_specs=vmem,
        out_shape=jax.ShapeDtypeStruct((groups, 8, rank * rank // groups + LANES), jnp.float32),
        scratch_shapes=[pltpu.VMEM((2 * rank, lists * slots), jnp.bfloat16), pltpu.VMEM((lists, rank, rank), jnp.float32)],
        compiler_params=pltpu.CompilerParams(vmem_limit_bytes=32 << 20),
        name="sketch_terms",
    )(where, rights, left_a, left_b)


def score_kernel(*refs):
    sketches, queries, out = refs[:-2], refs[-2], refs[-1]
    count = queries.shape[0]
    value = jnp.concatenate([s[...] for s in sketches], axis=0)
    head = value.astype(jnp.bfloat16)
    both = jnp.concatenate([head, (value - head.astype(jnp.float32)).astype(jnp.bfloat16)], axis=0)
    full = lax.dot_general(both, queries[...], NT, preferred_element_type=jnp.float32)
    rows = value.shape[0]
    terms = full[:rows] + full[rows:]
    squares = jnp.sum(value * value, axis=1, keepdims=True)
    scaled, exponent = leveled(terms)
    square, power = leveled(squares)
    lane = lax.broadcasted_iota(jnp.int32, (rows, LANES), 1)
    notes = jnp.where(lane == 0, exponent, jnp.where(lane == 1, square, power))
    for group in range(len(sketches)):
        out[group, :, :count] = scaled[group * 8:group * 8 + 8]
        out[group, :, count:] = notes[group * 8:group * 8 + 8]


def score_terms(sketches, queries):
    vmem = pl.BlockSpec(memory_space=pltpu.VMEM)
    return pl.pallas_call(
        score_kernel,
        in_specs=[vmem] * (len(sketches) + 1),
        out_specs=vmem,
        out_shape=jax.ShapeDtypeStruct((len(sketches), 8, queries.shape[0] + LANES), jnp.float32),
        compiler_params=pltpu.CompilerParams(vmem_limit_bytes=40 << 20),
        name="score_terms",
    )(*sketches, queries)


def ring(size, shift):
    return [(i, (i + shift) % size) for i in range(size)]


def decoded(coded, rank):
    wide = coded.astype(jnp.float32)
    return wide[..., :rank, :] * jnp.exp2(wide[..., rank:rank + 1, :] - TOP)


def local_square(activations, out_grads, lengths, proj_in, proj_out, queries):
    lists, slots, _ = activations.shape
    rank = proj_in.shape[1]
    groups = lax.axis_size("tensor")
    me = lax.axis_index("tensor")
    shifts = range(1, groups)
    tokens = lists * slots
    block = tokens // groups

    right = project_right(out_grads, proj_out.T)
    right, proj_in = lax.optimization_barrier((right, proj_in))
    coded = right.astype(jnp.float16)

    def part(shift):
        return lax.dynamic_slice_in_dim(coded, (me + shift) % groups * block, block, 1)

    arrived = [lax.ppermute(part(shift), "tensor", ring(groups, shift)) for shift in shifts]
    early = lists // 2
    left_a = project_left(activations, proj_in.T, lengths, 0, early)
    pieces = [part(0)] + arrived
    wide = [p.astype(jnp.float32) for p in pieces]
    summed = sum(w * jnp.exp2(w[rank:rank + 1] - TOP) for w in wide)
    exponent = functools.reduce(jnp.maximum, [w[rank:rank + 1] for w in wide]) + (groups - 1).bit_length()
    row = lax.broadcasted_iota(jnp.int32, summed.shape, 0)
    mine = jnp.where(row < rank, summed * jnp.exp2(TOP - exponent), exponent).astype(jnp.float16)
    mine, later = lax.optimization_barrier((mine, lengths))
    blocks = [mine] + [lax.ppermute(mine, "tensor", ring(groups, shift)) for shift in shifts]
    left_b = project_left(activations, proj_in.T, later, early, lists - early)
    rights = decoded(jnp.stack(blocks), rank)
    where = (me - jnp.arange(groups, dtype=jnp.int32)) % groups
    terms = sketch_terms(where, rights, left_a, left_b, lists, slots, groups)

    def towards(array, index):
        return lax.dynamic_index_in_dim(array, index, 0, keepdims=False)

    terms, queries = lax.optimization_barrier((terms, queries))
    coded = terms.astype(jnp.float16)
    entries = rank * rank // groups
    sketch = None
    for shift in range(groups):
        piece = towards(coded, (me + shift) % groups)
        if shift:
            piece = lax.ppermute(piece, "tensor", ring(groups, shift))
        piece = piece.astype(jnp.float32)
        piece = piece[:, :entries] * jnp.exp2(piece[:, entries:entries + 1] - TOP)
        sketch = piece if sketch is None else sketch + piece
    sketches = [sketch] + [lax.ppermute(sketch, "example", ring(groups, shift)) for shift in shifts]
    scores = score_terms(sketches, queries).astype(jnp.float16)
    count = queries.shape[0]
    here = lax.axis_index("example")
    final, square = 0.0, 0.0
    for shift in range(groups):
        target = (me + shift) % groups
        pairs = [
            (t * groups + e, e * groups + (t + shift) % groups)
            for t in range(groups) for e in range(groups)
        ]
        moved = lax.ppermute(towards(scores, (here - target) % groups), ("tensor", "example"), pairs).astype(jnp.float32)
        final += moved[:lists, :count] * jnp.exp2(moved[:lists, count:count + 1] - TOP)
        square += moved[:lists, count + 1:count + 2] * jnp.exp2(moved[:lists, count + 2:count + 3] - TOP)
    return final * lax.rsqrt(square + 1e-06)


def local(activations, out_grads, lengths, proj_in, proj_out, queries):
    nlists, slots, hidden_width = activations.shape
    feature_width = out_grads.shape[2]
    rank = proj_in.shape[1]
    left_part = jnp.dot(
        activations.reshape(nlists * slots, hidden_width),
        proj_in,
        preferred_element_type=jnp.float32,
    )
    right_part = jnp.dot(
        out_grads.reshape(nlists * slots, feature_width),
        proj_out,
        preferred_element_type=jnp.float32,
    )
    stacked = jnp.concatenate([left_part, right_part], axis=1).reshape(nlists, slots, 2 * rank)
    groups = lax.axis_size("tensor")
    block_rows = rank // groups
    summed = lax.psum(stacked, "tensor")
    positions = lax.broadcasted_iota(jnp.int32, (nlists, slots), 1)
    keep = (positions < lengths[:, None]).astype(jnp.float32)[:, :, None]
    left_full = summed[:, :, :rank] * keep
    right_full = summed[:, :, rank:]
    sketch = jnp.einsum("ltr,lts->lrs", left_full, right_full, precision=lax.Precision.HIGHEST)
    totals = jnp.sum(sketch * sketch, axis=(1, 2))
    unit_all = (sketch / jnp.sqrt(totals + 1e-06)[:, None, None]).astype(jnp.bfloat16)
    first_row = lax.axis_index("tensor") * block_rows
    mine = lax.dynamic_slice_in_dim(unit_all, first_row, block_rows, 1)
    mine = mine.reshape(nlists, block_rows * rank)
    terms = lax.dot_general(
        mine,
        lax.all_gather(queries, "example", axis=0, tiled=True),
        (((1,), (1,)), ((), ())),
        preferred_element_type=jnp.float32,
    )
    return lax.psum_scatter(terms, "tensor", scatter_dimension=1, tiled=True)


def solution(mesh):
    in_specs = (
        P(("parts", "example"), None, "tensor"),
        P(("parts", "example"), None, "tensor"),
        P(("parts", "example")),
        P("tensor", None),
        P("tensor", None),
        P(("parts", "example"), "tensor"),
    )
    out_specs = P(("parts", "example"), "tensor")
    square = mesh.shape["tensor"] == mesh.shape["example"]
    plan = local_square if square else local
    return jax.shard_map(plan, mesh=mesh, in_specs=in_specs, out_specs=out_specs, check_vma=False)
```

```python
import functools

import jax
import jax.numpy as jnp
from jax import lax
from jax.experimental import pallas as pl
from jax.experimental.pallas import tpu as pltpu
from jax.sharding import PartitionSpec as P

TOP = 14.0
EXTRA = 8
AHEAD = 3
LANES = 128
UNITS = 4
NT = (((1,), (1,)), ((), ()))
NN = (((1,), (0,)), ((), ()))


def leveled(value):
    largest = jnp.max(jnp.abs(value), axis=1, keepdims=True)
    exponent = jnp.ceil(jnp.log2(jnp.maximum(largest, 1e-30)))
    return value * jnp.exp2(TOP - exponent), exponent


def right_kernel(grads, basis, out, held, weights, arrived):
    rank = basis.shape[0]
    lists, slots = held.shape[:2]
    load = pltpu.make_async_copy(basis, weights, arrived.at[lists])
    load.start()

    def copy(l):
        return pltpu.make_async_copy(grads.at[l], held.at[l], arrived.at[l])

    for l in range(min(AHEAD, lists)):
        copy(l).start()
    load.wait()

    def step(l, carry):
        copy(l).wait()

        @pl.when(l + AHEAD < lists)
        def _():
            copy(l + AHEAD).start()

        right = lax.dot_general(held[l], weights[...], NT, preferred_element_type=jnp.float32).T
        largest = jnp.max(jnp.abs(right), axis=0, keepdims=True)
        exponent = jnp.ceil(jnp.log2(jnp.maximum(largest, 1e-30)))
        columns = pl.ds(pl.multiple_of(l * slots, slots), slots)
        out[:rank, columns] = right * jnp.exp2(TOP - exponent)
        out[rank:, columns] = jnp.broadcast_to(exponent, (EXTRA, slots))
        return carry

    lax.fori_loop(0, lists, step, 0)


def project_right(out_grads, basis):
    slots, width = out_grads.shape[1:]
    rank = basis.shape[0]
    tokens = out_grads.shape[0] * slots
    pieces = out_grads.reshape(tokens // slots, slots, width)
    return pl.pallas_call(
        right_kernel,
        in_specs=[pl.BlockSpec(memory_space=pltpu.HBM)] * 2,
        out_specs=pl.BlockSpec(memory_space=pltpu.VMEM),
        out_shape=jax.ShapeDtypeStruct((rank + EXTRA, tokens), jnp.float32),
        scratch_shapes=[
            pltpu.VMEM(pieces.shape, out_grads.dtype),
            pltpu.VMEM(basis.shape, basis.dtype),
            pltpu.SemaphoreType.DMA((pieces.shape[0] + 1,)),
        ],
        cost_estimate=pl.CostEstimate(flops=8 * tokens * width * rank, bytes_accessed=2 * out_grads.size, transcendentals=0),
        compiler_params=pltpu.CompilerParams(vmem_limit_bytes=52 << 20),
        name="project_right",
    )(pieces, pltpu.with_memory_space_constraint(basis, pltpu.HBM))


def left_kernel(first, slots, lengths, acts, basis, out, held, arrived):
    rank = basis.shape[0]
    depth, size = held.shape[:2]
    pieces = arrived.shape[1]
    rows, unit = size // pieces, size // UNITS
    steps = out.shape[0] // size
    cuts = slots // size

    def count_of(n):
        return lengths[first + n // cuts] - n % cuts * size

    def each(n, slot, act):
        count = count_of(n)
        for piece in range(pieces):
            @pl.when(piece * rows < count)
            def _():
                source = pl.ds(pl.multiple_of(n % cuts * size + piece * rows, rows), rows)
                act(pltpu.make_async_copy(acts.at[first + n // cuts, source, :], held.at[slot, pl.ds(piece * rows, rows), :], arrived.at[slot, piece]))

    for n in range(min(depth, steps)):
        each(n, n, lambda copy: copy.start())
    out[...] = jnp.zeros_like(out)

    def step(n, carry):
        slot = lax.rem(n, depth)
        each(n, slot, lambda copy: copy.wait())
        count = count_of(n)
        needed = jnp.minimum((count + unit - 1) // unit, UNITS)
        for units in range(1, UNITS + 1):
            @pl.when(needed == units)
            def _():
                left = lax.dot_general(held[slot, :units * unit, :], basis[...], NT, preferred_element_type=jnp.float32)
                row = lax.broadcasted_iota(jnp.int32, left.shape, 0)
                left = jnp.where(row < count, left, 0.0)
                head = left.astype(jnp.bfloat16)
                place = pl.ds(pl.multiple_of(n * size, size), units * unit)
                out[place, :rank] = head
                out[place, rank:] = (left - head.astype(jnp.float32)).astype(jnp.bfloat16)

        @pl.when(n + depth < steps)
        def _():
            each(n + depth, slot, lambda copy: copy.start())
        return carry

    lax.fori_loop(0, steps, step, 0)


def project_left(activations, basis, lengths, first, lists):
    slots, width = activations.shape[1:]
    rank = basis.shape[0]
    size, depth = 256, 4
    return pl.pallas_call(
        functools.partial(left_kernel, first, slots),
        in_specs=[
            pl.BlockSpec(memory_space=pltpu.SMEM),
            pl.BlockSpec(memory_space=pl.ANY),
            pl.BlockSpec(memory_space=pltpu.VMEM),
        ],
        out_specs=pl.BlockSpec(memory_space=pltpu.VMEM),
        out_shape=jax.ShapeDtypeStruct((lists * slots, 2 * rank), jnp.bfloat16),
        scratch_shapes=[pltpu.VMEM((depth, size, width), activations.dtype), pltpu.SemaphoreType.DMA((depth, size // 64))],
        cost_estimate=pl.CostEstimate(flops=8 * lists * slots * width * rank, bytes_accessed=2 * lists * slots * width, transcendentals=0),
        compiler_params=pltpu.CompilerParams(vmem_limit_bytes=36 << 20),
        name="project_left",
    )(lengths, activations, basis)


def sketch_kernel(where, rights, left_a, left_b, out, both, sums):
    out[...] = jnp.zeros_like(out)
    lists, rank = sums.shape[:2]
    width = rights.shape[2]
    slots = both.shape[1] // lists
    for block in range(rights.shape[0]):
        value = rights[block]
        head = value.astype(jnp.bfloat16)
        columns = pl.ds(pl.multiple_of(where[block] * width, width), width)
        both[:rank, columns] = head
        both[rank:, columns] = (value - head.astype(jnp.float32)).astype(jnp.bfloat16)
    early = left_a.shape[0] // slots
    for l in range(lists):
        left = left_a[l * slots:(l + 1) * slots] if l < early else left_b[(l - early) * slots:(l - early + 1) * slots]
        full = lax.dot_general(both[:, l * slots:(l + 1) * slots], left, NN, preferred_element_type=jnp.float32)
        side = full[:rank] + full[rank:]
        sums[l] = (side[:, :rank] + side[:, rank:]).T
    rows = rank // out.shape[0]
    for i in range(rank):
        column = (i % rows) * rank
        out[i // rows, :lists, column:column + rank] = sums[:, i, :]
    for group in range(out.shape[0]):
        scaled, exponent = leveled(out[group, :lists, :rows * rank])
        out[group, :lists, :rows * rank] = scaled
        out[group, :lists, rows * rank:] = jnp.broadcast_to(exponent, (lists, LANES))


def sketch_terms(where, rights, left_a, left_b, lists, slots, groups):
    rank = rights.shape[1]
    vmem = pl.BlockSpec(memory_space=pltpu.VMEM)
    return pl.pallas_call(
        sketch_kernel,
        in_specs=[pl.BlockSpec(memory_space=pltpu.SMEM), vmem, vmem, vmem],
        out_specs=vmem,
        out_shape=jax.ShapeDtypeStruct((groups, 8, rank * rank // groups + LANES), jnp.float32),
        scratch_shapes=[pltpu.VMEM((2 * rank, lists * slots), jnp.bfloat16), pltpu.VMEM((lists, rank, rank), jnp.float32)],
        compiler_params=pltpu.CompilerParams(vmem_limit_bytes=32 << 20),
        name="sketch_terms",
    )(where, rights, left_a, left_b)


def score_kernel(*refs):
    sketches, queries, out = refs[:-2], refs[-2], refs[-1]
    count = queries.shape[0]
    value = jnp.concatenate([s[...] for s in sketches], axis=0)
    head = value.astype(jnp.bfloat16)
    both = jnp.concatenate([head, (value - head.astype(jnp.float32)).astype(jnp.bfloat16)], axis=0)
    full = lax.dot_general(both, queries[...], NT, preferred_element_type=jnp.float32)
    rows = value.shape[0]
    terms = full[:rows] + full[rows:]
    squares = jnp.sum(value * value, axis=1, keepdims=True)
    scaled, exponent = leveled(terms)
    square, power = leveled(squares)
    lane = lax.broadcasted_iota(jnp.int32, (rows, LANES), 1)
    notes = jnp.where(lane == 0, exponent, jnp.where(lane == 1, square, power))
    for group in range(len(sketches)):
        out[group, :, :count] = scaled[group * 8:group * 8 + 8]
        out[group, :, count:] = notes[group * 8:group * 8 + 8]


def score_terms(sketches, queries):
    vmem = pl.BlockSpec(memory_space=pltpu.VMEM)
    return pl.pallas_call(
        score_kernel,
        in_specs=[vmem] * (len(sketches) + 1),
        out_specs=vmem,
        out_shape=jax.ShapeDtypeStruct((len(sketches), 8, queries.shape[0] + LANES), jnp.float32),
        compiler_params=pltpu.CompilerParams(vmem_limit_bytes=40 << 20),
        name="score_terms",
    )(*sketches, queries)


def ring(size, shift):
    return [(i, (i + shift) % size) for i in range(size)]


def decoded(coded, rank):
    wide = coded.astype(jnp.float32)
    return wide[..., :rank, :] * jnp.exp2(wide[..., rank:rank + 1, :] - TOP)


def local_square(activations, out_grads, lengths, proj_in, proj_out, queries):
    lists, slots, _ = activations.shape
    rank = proj_in.shape[1]
    groups = lax.axis_size("tensor")
    me = lax.axis_index("tensor")
    shifts = range(1, groups)
    tokens = lists * slots
    block = tokens // groups

    right = project_right(out_grads, proj_out.T)
    coded = right.astype(jnp.float16)

    def part(shift):
        return lax.dynamic_slice_in_dim(coded, (me + shift) % groups * block, block, 1)

    arrived = [lax.ppermute(part(shift), "tensor", ring(groups, shift)) for shift in shifts]
    early = lists // 2
    left_a = project_left(activations, proj_in.T, lengths, 0, early)
    pieces = [part(0)] + arrived
    wide = [p.astype(jnp.float32) for p in pieces]
    summed = sum(w * jnp.exp2(w[rank:rank + 1] - TOP) for w in wide)
    exponent = functools.reduce(jnp.maximum, [w[rank:rank + 1] for w in wide]) + (groups - 1).bit_length()
    row = lax.broadcasted_iota(jnp.int32, summed.shape, 0)
    mine = jnp.where(row < rank, summed * jnp.exp2(TOP - exponent), exponent).astype(jnp.float16)
    mine, later = lax.optimization_barrier((mine, lengths))
    blocks = [mine] + [lax.ppermute(mine, "tensor", ring(groups, shift)) for shift in shifts]
    left_b = project_left(activations, proj_in.T, later, early, lists - early)
    rights = decoded(jnp.stack(blocks), rank)
    where = (me - jnp.arange(groups, dtype=jnp.int32)) % groups
    terms = sketch_terms(where, rights, left_a, left_b, lists, slots, groups)

    def towards(array, index):
        return lax.dynamic_index_in_dim(array, index, 0, keepdims=False)

    coded = terms.astype(jnp.float16)
    entries = rank * rank // groups
    sketch = None
    for shift in range(groups):
        piece = towards(coded, (me + shift) % groups)
        if shift:
            piece = lax.ppermute(piece, "tensor", ring(groups, shift))
        piece = piece.astype(jnp.float32)
        piece = piece[:, :entries] * jnp.exp2(piece[:, entries:entries + 1] - TOP)
        sketch = piece if sketch is None else sketch + piece
    sketches = [sketch] + [lax.ppermute(sketch, "example", ring(groups, shift)) for shift in shifts]
    scores = score_terms(sketches, queries).astype(jnp.float16)
    count = queries.shape[0]
    here = lax.axis_index("example")
    final, square = 0.0, 0.0
    for shift in range(groups):
        target = (me + shift) % groups
        pairs = [
            (t * groups + e, e * groups + (t + shift) % groups)
            for t in range(groups) for e in range(groups)
        ]
        moved = lax.ppermute(towards(scores, (here - target) % groups), ("tensor", "example"), pairs).astype(jnp.float32)
        final += moved[:lists, :count] * jnp.exp2(moved[:lists, count:count + 1] - TOP)
        square += moved[:lists, count + 1:count + 2] * jnp.exp2(moved[:lists, count + 2:count + 3] - TOP)
    return final * lax.rsqrt(square + 1e-06)


def local(activations, out_grads, lengths, proj_in, proj_out, queries):
    nlists, slots, hidden_width = activations.shape
    feature_width = out_grads.shape[2]
    rank = proj_in.shape[1]
    left_part = jnp.dot(
        activations.reshape(nlists * slots, hidden_width),
        proj_in,
        preferred_element_type=jnp.float32,
    )
    right_part = jnp.dot(
        out_grads.reshape(nlists * slots, feature_width),
        proj_out,
        preferred_element_type=jnp.float32,
    )
    stacked = jnp.concatenate([left_part, right_part], axis=1).reshape(nlists, slots, 2 * rank)
    groups = lax.axis_size("tensor")
    block_rows = rank // groups
    summed = lax.psum(stacked, "tensor")
    positions = lax.broadcasted_iota(jnp.int32, (nlists, slots), 1)
    keep = (positions < lengths[:, None]).astype(jnp.float32)[:, :, None]
    left_full = summed[:, :, :rank] * keep
    right_full = summed[:, :, rank:]
    sketch = jnp.einsum("ltr,lts->lrs", left_full, right_full, precision=lax.Precision.HIGHEST)
    totals = jnp.sum(sketch * sketch, axis=(1, 2))
    unit_all = (sketch / jnp.sqrt(totals + 1e-06)[:, None, None]).astype(jnp.bfloat16)
    first_row = lax.axis_index("tensor") * block_rows
    mine = lax.dynamic_slice_in_dim(unit_all, first_row, block_rows, 1)
    mine = mine.reshape(nlists, block_rows * rank)
    terms = lax.dot_general(
        mine,
        lax.all_gather(queries, "example", axis=0, tiled=True),
        (((1,), (1,)), ((), ())),
        preferred_element_type=jnp.float32,
    )
    return lax.psum_scatter(terms, "tensor", scatter_dimension=1, tiled=True)


def solution(mesh):
    in_specs = (
        P(("parts", "example"), None, "tensor"),
        P(("parts", "example"), None, "tensor"),
        P(("parts", "example")),
        P("tensor", None),
        P("tensor", None),
        P(("parts", "example"), "tensor"),
    )
    out_specs = P(("parts", "example"), "tensor")
    square = mesh.shape["tensor"] == mesh.shape["example"]
    plan = local_square if square else local
    return jax.shard_map(plan, mesh=mesh, in_specs=in_specs, out_specs=out_specs, check_vma=False)
```
